1024 devices in a mesh: ep: 16 (over x, y), tp: 64 (over z, core).
Axes of the slice: x: 4, y: 4, z: 32, core: 2. Of those that a mesh axis runs over, the one named last changes fastest.
Arguments:
- grad_out: bfloat16 [16384, 3584], P('tp', 'ep'), may hold values from -6 to 6
- route_probs: float32 [16384, 2], P('tp'), may hold values from 0.2 to 1
- routes: int32 [16384, 2], P('tp'), may hold values from 0 to 63, all different within a row; in each aligned block of 256 rows (0 to 255, 256 to 511, ...) at most 12 rows name the same one
- saved_up: bfloat16 [64, 2432, 768], P('tp', 'ep'), may hold values from -6 to 6
- w_up: bfloat16 [64, 3584, 2432], P('tp', 'ep'), may hold values from -0.09375 to 0.09375
- w_down: bfloat16 [64, 2432, 3584], P('tp', None, 'ep'), may hold values from -0.125 to 0.125
Outputs:
- input_grad: bfloat16 [16384, 3584], P('tp', 'ep')
The draws below stay inside these ranges and needn't reach their ends.
Inputs may be any that keep to these rules, and one draw needn't show every extreme that they name: `routes`: the two experts of a row differ. In each aligned block of 256 rows no expert is named by more than 12 rows, a bound that some block reaches.
All inputs are finite; a program needn't handle non-finite values.
Results may differ from the reference program's by a relative error of at most 0.023.
Values may be sent and summed in bfloat16 or wider, within the bound.
A program may use at most 32 MiB of HBM per device.

```python
import math
import jax
import jax.numpy as jnp
import numpy as np
from jax import lax

D = 3584
FF = 2432
TOK_DEV = 256
EXPERTS = 64
CAP = 12
SLOTS = 768
TOKENS = 16384
N_EP = 16
N_TP = 64


def level_of(key, dims, shards, low, largest):
    gain = 1.0
    for dim, shards_of in shards:
        steps = jax.random.uniform(jax.random.fold_in(jax.random.fold_in(key, 6), dim), (shards_of,), jnp.float32, low / len(shards), largest / len(shards))
        gain = gain * jnp.repeat(jnp.exp(steps), dims[dim] // shards_of).reshape((-1,) + (1,) * (len(dims) - 1 - dim))
    return gain


def shared_out(key, own, number, rows, number_of, top, reach, slope):
    order = jax.random.permutation(key, number_of)
    crowded, usual = shares(number_of, rows * top, reach, slope, True), shares(number_of, rows * top, reach, slope, False)
    places = jnp.arange(number_of)

    def named(tallies, offset_by):
        used = int((tallies > 0).sum())
        fixed = max(1, used // 4)
        shifted = fixed + (places - fixed + offset_by * (used - fixed)) % max(1, number_of - fixed)
        return jnp.zeros((number_of,), jnp.int32).at[order[jnp.where(places < fixed, places, shifted)]].set(jnp.asarray(tallies, jnp.int32))

    tallies = jnp.where(number % 4 == 0, named(crowded, number // 4), named(usual, number - number // 4 - 1))
    mixed = jax.random.permutation(jax.random.fold_in(own, 3), number_of)
    giver, receiver = mixed[0:number_of // 2 * 2:2], mixed[1:number_of // 2 * 2:2]
    slack = jnp.minimum(tallies[giver] - 1, reach - tallies[receiver]) // 2
    slack = jnp.where((giver == order[0]) | (receiver == order[0]) | (tallies[receiver] == 0), 0, jnp.maximum(slack, 0))
    shifted = jax.random.randint(jax.random.fold_in(own, 4), (number_of // 2,), 0, 1 << 20) % (slack + 1)
    tallies = tallies.at[giver].add(-shifted).at[receiver].add(shifted)
    labels = jnp.searchsorted(jnp.cumsum(tallies), jnp.arange(rows * top), side="right").astype(jnp.int32)
    grid = labels.reshape(top, rows).T
    grid = grid[jax.random.permutation(jax.random.fold_in(own, 1), rows)]
    offset_by = jax.random.randint(jax.random.fold_in(own, 2), (rows, 1), 0, top)
    return jnp.take_along_axis(grid, (jnp.arange(top)[None, :] + offset_by) % top, axis=1)


def shares(number_of, total, reach, lean, full):
    portions = [(1 << 20) // math.isqrt(rank ** lean) + 1 for rank in range(1, number_of + 1)]
    largest = reach if full else min(reach, max(-(-total // number_of), total * portions[0] // sum(portions)))
    least = 1 if total - largest >= number_of - 1 else 0
    holding, rest = [largest] + [least] * (number_of - 1), total - largest - least * (number_of - 1)
    while rest > 0:
        movable = [i for i in range(1, number_of) if holding[i] < largest] or [i for i in range(1, number_of) if holding[i] < reach]
        pool, remaining = sum([portions[i] for i in movable]), rest
        for i in movable:
            extra = min(reach - holding[i], max(1, remaining * portions[i] // pool), rest)
            holding[i] = holding[i] + extra
            rest = rest - extra
    return np.array(holding)


def scatter_about(key, shape, deviation, limit, pieces=(), kind=jnp.bfloat16):
    drawn = jax.random.normal(key, shape, jnp.float32) * deviation
    if len(pieces) > 0:
        drawn = level_of(key, shape, pieces, -0.22, 0.18) * drawn
    return jnp.clip(drawn, min=-limit, max=limit).astype(kind)


def setup_inputs(seed: int = 0) -> dict:
    keys = jax.random.split(jax.random.key(seed), 7)
    grad_out = scatter_about(keys[0], (TOKENS, D), 1.0, 6.0, ((0, 64), (1, 16)))
    route_probs = jnp.clip(0.2 + 0.8 * jax.random.uniform(keys[1], (TOKENS, 2), jnp.float32) ** level_of(keys[1], (TOKENS, 2), ((0, 64),), -0.2, 0.2), 0.2, 1.0)
    routes_keys = jax.random.split(jax.random.fold_in(keys[2], 1), TOKENS // TOK_DEV)
    routes_turns = jax.random.permutation(jax.random.fold_in(keys[2], 3), TOKENS // TOK_DEV)
    routes = jax.vmap(lambda own, number: shared_out(jax.random.fold_in(keys[2], 2), own, number, TOK_DEV, EXPERTS, 2, CAP, 2))(routes_keys, routes_turns).reshape((TOKENS, 2))
    saved_up = scatter_about(keys[3], (EXPERTS, FF, SLOTS), 1.5, 6.0, ((0, 64), (1, 16)))
    w_up = scatter_about(keys[4], (EXPERTS, D, FF), D ** -0.5, 0.09375, ((0, 64), (1, 16)))
    w_down = scatter_about(keys[5], (EXPERTS, FF, D), FF ** -0.5, 0.125, ((0, 64), (2, 16)))
    return {"grad_out": grad_out, "route_probs": route_probs, "routes": routes, "saved_up": saved_up, "w_up": w_up, "w_down": w_down}


def reference(grad_out, route_probs, routes, saved_up, w_up, w_down):
    blocked = routes.reshape(N_TP, 2 * TOK_DEV)
    experts_iota = jnp.arange(EXPERTS, dtype=jnp.int32)
    onehot = (blocked[:, :, None] == experts_iota[None, None, :]).astype(jnp.int32)
    before = jnp.cumsum(onehot, axis=1) - onehot
    earlier = jnp.sum(before * onehot, axis=2).astype(jnp.int32)
    slot = (jnp.arange(N_TP, dtype=jnp.int32)[:, None] * CAP + earlier).reshape(-1)
    flat_routes = routes.reshape(-1)
    pair_total = 2 * TOKENS
    slot_table = jnp.full((EXPERTS * SLOTS,), pair_total, dtype=jnp.int32)
    slot_table = slot_table.at[flat_routes * SLOTS + slot].set(jnp.arange(pair_total, dtype=jnp.int32))
    flat_probs = route_probs.reshape(-1)
    block_width = D // N_EP

    def per_expert(running, expert):
        pair_index = lax.dynamic_slice_in_dim(slot_table, (expert * SLOTS).astype(jnp.int32), SLOTS)
        occupied = pair_index < pair_total
        clipped = jnp.minimum(pair_index, pair_total - 1)
        token_index = clipped // 2
        dispatched = jnp.where(occupied[:, None], grad_out[token_index], 0.0).astype(jnp.bfloat16)
        down_mat = w_down[expert].astype(jnp.float32).reshape(FF, N_EP, block_width)
        partials = jnp.einsum("fbd,sbd->bfs", down_mat, dispatched.astype(jnp.float32).reshape(SLOTS, N_EP, block_width))
        rounded = lax.optimization_barrier(partials.astype(jnp.bfloat16)).astype(jnp.float32)
        hidden_grad = jnp.sum(rounded, axis=0)
        saved = saved_up[expert].astype(jnp.float32)
        gate_value = jax.nn.sigmoid(saved)
        grad_up = (hidden_grad * gate_value * (1.0 + saved * (1.0 - gate_value))).astype(jnp.bfloat16)
        expert_grad = jnp.dot(w_up[expert], grad_up, preferred_element_type=jnp.float32).astype(jnp.bfloat16)
        weights = jnp.where(occupied, flat_probs[clipped], 0.0)
        contrib = expert_grad.astype(jnp.float32).T * weights[:, None]
        target = jnp.where(occupied, token_index, TOKENS).astype(jnp.int32)
        running = running.at[target].add(contrib, mode="drop")
        return running, None

    start_value = jnp.zeros((TOKENS, D), dtype=jnp.float32)
    accumulated, _ = lax.scan(per_expert, start_value, jnp.arange(EXPERTS, dtype=jnp.int32))
    return accumulated.astype(jnp.bfloat16)
```

```python
import functools
import jax
import jax.numpy as jnp
from jax import lax
from jax.experimental import pallas as pl
from jax.experimental.pallas import tpu as pltpu
from jax.sharding import PartitionSpec as P

MESH = pl.DeviceIdType.MESH
F32 = jnp.float32
BF16 = jnp.bfloat16

CHIPS = 32
AWAY = [(-(p // 2) if p % 2 == 0 else (p + 1) // 2) % CHIPS for p in range(CHIPS)]
PLACE = [AWAY.index(r) for r in range(CHIPS)]
BACK = [PLACE[-r % CHIPS] for r in AWAY]
OWN = PLACE[0]
CAP = 12
PAIR = 2 * CAP
SLOTS = CHIPS * PAIR
TOK = 256
WIDTH = 224
LANES = 256
HID = 152
HALF = 80
CHUNKS = 6
CHUNK = SLOTS // CHUNKS
READY = [0, 6, 12, 18, 24, 30]
PARTS = (0, 384, 512, 768)


def nt_dot(a, b):
    return lax.dot_general(a, b, (((1,), (1,)), ((), ())), preferred_element_type=F32)


def to_message(rows):
    n = rows.shape[0] // PAIR
    blocks = rows.reshape(n, PAIR, LANES)
    return jnp.concatenate([blocks[:, :, :128], blocks[:, :, 128:]], axis=1).astype(BF16)


def from_message(message):
    wide = message.astype(F32)
    rows = jnp.concatenate([wide[:, :PAIR], wide[:, PAIR:]], axis=2)
    return rows.reshape(rows.shape[0] * PAIR, LANES)


def look_up(table, index):
    found = jnp.zeros_like(index)
    for i, value in enumerate(table):
        found = jnp.where(index == i, value, found)
    return found


def whole(k):
    return -(-k * CHUNK // PAIR)


def done(k):
    return k * CHUNK // PAIR


def kernel(
    grad_ref, route_ref, prob_ref, down_hbm, up_hbm, saved_hbm, out_ref,
    grads, routes, probs, down_in, up, saved, down,
    send, got, back, came, x32, y32, part, in_a, in_b, in_c, run, in_a2, in_b2, in_c2, gath, gu, eg,
    factor, picks, cols, mine, theirs,
    ls, zs, zr, rs, rr, xs, xr, fs, fr,
):
    ep = lax.axis_index("ep")
    me = lax.axis_index("tp")
    z = lax.div(me, 2)
    c = lax.rem(me, 2)
    x = lax.div(ep, 4)
    y = lax.rem(ep, 4)
    s = 1 - 2 * c
    sibling = (ep, 2 * z + 1 - c)

    def chip(r):
        return (ep, lax.rem(z + r, CHIPS) * 2 + c)

    def near(o, phase, coord):
        along_x = (o == 0) == (phase == 0)
        return (coord * 4 + y if along_x else x * 4 + coord, me)

    def ring(coord):
        return lax.rem(coord + s + 4, 4), lax.rem(coord - s + 4, 4), lax.rem(coord + 2, 4)

    barrier = pltpu.get_barrier_semaphore()

    def greet(r, carry):
        pl.semaphore_signal(barrier, inc=1, device_id=chip(r), device_id_type=MESH)
        return carry

    lax.fori_loop(1, CHIPS, greet, 0)
    pl.semaphore_signal(barrier, inc=1, device_id=sibling, device_id_type=MESH)
    for o in range(2):
        for step in (1, 2, 3):
            peer = near(o, 0, lax.rem((x if o == 0 else y) + step, 4))
            pl.semaphore_signal(barrier, inc=1, device_id=peer, device_id_type=MESH)
    loads = [
        pltpu.make_async_copy(src, dst, ls.at[i])
        for i, (src, dst) in enumerate([(down_hbm, down_in), (saved_hbm, saved), (up_hbm, up)])
    ]
    for load in loads:
        load.start()
    pl.semaphore_wait(barrier, CHIPS - 1 + 1 + 6)

    trades = [
        pltpu.make_async_remote_copy(
            src_ref=src, dst_ref=dst.at[c], send_sem=fs.at[i], recv_sem=fr.at[i],
            device_id=sibling, device_id_type=MESH,
        )
        for i, (src, dst) in enumerate([(route_ref, routes), (prob_ref, probs), (grad_ref, grads)])
    ]
    for trade in trades:
        trade.start()
    grads[c] = grad_ref[...]
    routes[c] = route_ref[...]
    probs[c] = prob_ref[...]

    expert = lax.broadcasted_iota(jnp.int32, (64, 1), 0)
    away = ((expert >> 1) - z + CHIPS) & (CHIPS - 1)
    place_to = look_up(PLACE, away)
    place_from = look_up(BACK, place_to)
    base_to = jnp.where((expert & 1) == c, place_to * PAIR, -4096).astype(F32)
    base_from = jnp.where((expert & 1) == c, place_from * PAIR, -4096).astype(F32)
    experts = lax.broadcasted_iota(jnp.int32, (64, TOK), 0)
    earlier = jnp.where(
        lax.broadcasted_iota(jnp.int32, (TOK, TOK), 0) < lax.broadcasted_iota(jnp.int32, (TOK, TOK), 1),
        1.0, 0.0,
    ).astype(BF16)
    rows = lax.broadcasted_iota(jnp.int32, (SLOTS, TOK), 0).astype(F32)

    def tokens_of(block):
        route = routes[block]
        first = jnp.where(experts == route[0:1], 1.0, 0.0)
        second = jnp.where(experts == route[1:2], 1.0, 0.0)
        before = jnp.dot((first + second).astype(BF16), earlier, preferred_element_type=F32)
        shift = (CAP * block).astype(F32)
        one, two, one_from, two_from = [
            jnp.sum(hot * (before + base), axis=0, keepdims=True) + shift
            for base in (base_to, base_from)
            for hot in (first, second)
        ]
        hot = jnp.where((rows == one) | (rows == two), 1.0, 0.0).astype(BF16)
        wide = jnp.concatenate([grads[block], jnp.zeros((LANES - WIDTH, TOK), BF16)], axis=0)
        return nt_dot(hot, wide), [one_from, two_from, probs[block]]

    total, found = tokens_of(c)
    for trade in trades:
        trade.wait_recv()
    other, other_found = tokens_of(1 - c)
    send[...] = to_message(total + other)

    def dispatch(p, group):
        i = BACK[p]
        return pltpu.make_async_remote_copy(
            src_ref=send.at[i], dst_ref=got.at[p], send_sem=zs, recv_sem=zr.at[group],
            device_id=chip(AWAY[i]), device_id_type=MESH,
        )

    def send_back(p, group):
        return pltpu.make_async_remote_copy(
            src_ref=back.at[p], dst_ref=came.at[p], send_sem=rs, recv_sem=rr.at[group],
            device_id=chip(AWAY[p]), device_id_type=MESH,
        )

    def each_place(lo, hi, act):
        for p in range(lo, hi):
            if p != OWN:
                act(p)

    def group_ref(buffer, lo, hi):
        return buffer.at[lo:hi - (1 if lo <= OWN < hi else 0)]

    def group_arrived(buffer, lo, hi, sem):
        ref = group_ref(buffer, lo, hi)
        pltpu.make_async_remote_copy(
            src_ref=ref, dst_ref=ref, send_sem=zs, recv_sem=sem, device_id=sibling, device_id_type=MESH,
        ).wait_recv()

    def group_left(buffer, sem):
        ref = group_ref(buffer, 0, CHIPS)
        pltpu.make_async_remote_copy(
            src_ref=ref, dst_ref=ref, send_sem=sem, recv_sem=zr.at[0], device_id=sibling, device_id_type=MESH,
        ).wait_send()

    for k in range(CHUNKS):
        each_place(whole(k), whole(k + 1), lambda p, k=k: dispatch(p, k).start())
    got[OWN] = send[OWN]

    loads[0].wait()

    def turn(j, carry):
        at = pl.multiple_of(128 * j, 128)
        block = down_in[:, pl.ds(at, 128)].astype(F32)
        block = jnp.concatenate([block, jnp.zeros((LANES - WIDTH, 128), F32)], axis=0)
        down[pl.ds(at, 128), :] = block.T.astype(BF16)
        return carry

    lax.fori_loop(0, 16 * HID // 128, turn, 0)
    loads[1].wait()
    lane = lax.broadcasted_iota(jnp.int32, (1, SLOTS), 1)
    place = (lane * 2731) >> 16
    source = ((z + look_up(AWAY, place)) & (CHIPS - 1)) * PAIR + (lane - PAIR * place)
    order = jnp.where(
        lax.broadcasted_iota(jnp.int32, (SLOTS, SLOTS), 0) == source, 1.0, 0.0
    ).astype(BF16)
    u = jnp.dot(saved[...], order, preferred_element_type=F32)
    g = 1.0 / (1.0 + jnp.exp(-u))
    factor[0:HID] = g * (1.0 + u * (1.0 - g))
    factor[HID:] = jnp.zeros((2 * HALF - HID, SLOTS), F32)
    cols[...] = jnp.concatenate(found + other_found + [jnp.zeros((120, TOK), F32)], axis=0).T
    lanes = lax.broadcasted_iota(jnp.int32, (TOK, SLOTS), 1).astype(F32)
    for i, column in enumerate((0, 1, 4, 5)):
        picks[i] = jnp.where(lanes == cols[:, column:column + 1], 1.0, 0.0).astype(BF16)
    loads[2].wait()

    def transfers(k, o):
        a, b = (x, y) if o == 0 else (y, x)
        ap, am, a2 = ring(a)
        bp, bm, b2 = ring(b)
        ga = gath.at[k, o]
        return [
            (part.at[k, o, a2], in_a.at[k, o], near(o, 0, ap), in_a.at[k, o]),
            (part.at[k, o, am], in_b.at[k, o], near(o, 0, am), in_b.at[k, o]),
            (part.at[k, o, ap], in_c.at[k, o], near(o, 0, ap), in_c.at[k, o]),
            (run.at[k, o, bp], in_a2.at[k, o], near(o, 1, bp), in_a2.at[k, o]),
            (run.at[k, o, bm], in_b2.at[k, o], near(o, 1, bm), in_b2.at[k, o]),
            (run.at[k, o, b2], in_c2.at[k, o], near(o, 1, b2), in_c2.at[k, o]),
            (ga.at[a, b], ga.at[a, b], near(o, 1, bp), ga.at[a, bm]),
            (ga.at[a, b], ga.at[a, b], near(o, 1, bm), ga.at[a, bp]),
            (ga.at[a, b], ga.at[a, b], near(o, 1, b2), ga.at[a, b2]),
            (ga.at[a], ga.at[a], near(o, 0, ap), ga.at[am]),
            (ga.at[a], ga.at[a], near(o, 0, am), ga.at[ap]),
            (ga.at[am], ga.at[am], near(o, 0, ap), ga.at[a2]),
        ]

    def link(k, o, q, src, dst, peer):
        return pltpu.make_async_remote_copy(
            src_ref=src, dst_ref=dst, send_sem=xs.at[k, o, q], recv_sem=xr.at[k, o, q],
            device_id=peer, device_id_type=MESH,
        )

    def start(k, o, *qs):
        for q in qs:
            src, dst, peer, _ = transfers(k, o)[q]
            link(k, o, q, src, dst, peer).start()

    def arrived(k, o, *qs):
        for q in qs:
            _, _, peer, land = transfers(k, o)[q]
            link(k, o, q, land, land, peer).wait_recv()

    def left(k, o, *qs):
        for q in qs:
            src, dst, peer, _ = transfers(k, o)[q]
            link(k, o, q, src, dst, peer).wait_send()

    def stage0(k):
        lo, hi = whole(k), whole(k + 1)
        group_arrived(got, lo, hi, zr.at[k])
        x32[PAIR * lo:PAIR * hi] = from_message(got[lo:hi])
        tokens = x32[k * CHUNK:(k + 1) * CHUNK].astype(BF16)

        def pair(i, carry):
            weights = down[pl.ds(pl.multiple_of(2 * HID * i, 16), 2 * HID), :]
            hidden = nt_dot(weights, tokens)
            px = lax.div(i, 2)
            for j in range(2):
                py = 2 * lax.rem(i, 2) + j
                block = hidden[j * HID:(j + 1) * HID]
                part[k, 0, px, py] = block[0:HALF].astype(BF16)
                part[k, 1, py, px] = jnp.concatenate(
                    [block[HALF:], jnp.zeros((2 * HALF - HID, CHUNK), F32)], axis=0
                ).astype(BF16)
            return carry

        lax.fori_loop(0, 8, pair, 0)
        for o in range(2):
            start(k, o, 0, 1)

    def stage1(k):
        for o in range(2):
            ap, _, _ = ring(x if o == 0 else y)
            arrived(k, o, 0)
            part[k, o, ap] = (part[k, o, ap].astype(F32) + in_a[k, o].astype(F32)).astype(BF16)
            start(k, o, 2)

    def stage2(k):
        for o in range(2):
            arrived(k, o, 1, 2)
            a = x if o == 0 else y
            run[k, o] = (
                part[k, o, a].astype(F32) + in_b[k, o].astype(F32) + in_c[k, o].astype(F32)
            ).astype(BF16)
            start(k, o, 3, 4, 5)

    def stage3(k):
        for o in range(2):
            arrived(k, o, 3, 4, 5)
            a, b = (x, y) if o == 0 else (y, x)
            hidden = run[k, o, b].astype(F32) + in_a2[k, o].astype(F32)
            hidden = hidden + in_b2[k, o].astype(F32) + in_c2[k, o].astype(F32)
            slope = factor[o * HALF:(o + 1) * HALF, k * CHUNK:(k + 1) * CHUNK]
            gath[k, o, a, b] = (hidden * slope).astype(BF16)
            start(k, o, 6, 7, 8)

    def stage4(k):
        for o in range(2):
            arrived(k, o, 6, 7, 8)
            start(k, o, 9, 10)

    def stage5(k):
        for o in range(2):
            arrived(k, o, 9)
            start(k, o, 11)

    def stage6(k):
        for o in range(2):
            arrived(k, o, 10, 11)

        def pair(i, carry):
            px = lax.div(i, 2)
            pieces = []
            for j in range(2):
                py = 2 * lax.rem(i, 2) + j
                pieces.append(gath[k, 0, px, py].astype(F32))
                pieces.append(gath[k, 1, py, px].astype(F32)[0:HID - HALF])
            gu[pl.ds(pl.multiple_of(2 * HID * i, 16), 2 * HID), :] = jnp.concatenate(pieces, axis=0).astype(BF16)
            return carry

        lax.fori_loop(0, 8, pair, 0)
        result = jnp.dot(up[...], gu[...], preferred_element_type=F32)
        padded = jnp.concatenate([result, jnp.zeros((LANES - WIDTH, CHUNK), F32)], axis=0)
        eg[k * CHUNK:(k + 1) * CHUNK] = padded.T
        lo, hi = done(k), done(k + 1)
        back[lo:hi] = to_message(eg[PAIR * lo:PAIR * hi])
        each_place(lo, hi, lambda p: send_back(p, k).start())
        if lo <= OWN < hi:
            came[OWN] = back[OWN]
        for o in range(2):
            left(k, o, *range(12))

    stages = [stage0, stage1, stage2, stage3, stage4, stage5, stage6]
    offsets = [0, 4, 7, 10.5, 13.5, 17.5, 20.5]
    plan = sorted((READY[k] + offsets[i], k, i) for k in range(CHUNKS) for i in range(len(stages)))
    for _, k, i in plan:
        stages[i](k)
    group_left(send, zs)
    for trade in trades:
        trade.wait_send()

    sums = [None, None]
    taken = 0
    for lo, hi in zip(PARTS[:-1], PARTS[1:]):
        while done(taken) * PAIR < hi:
            first, last = done(taken), done(taken + 1)
            group_arrived(came, first, last, rr.at[taken])
            y32[PAIR * first:PAIR * last] = from_message(came[first:last])
            taken += 1
        slots = y32[lo:hi].astype(BF16)
        for i in range(2):
            for k in range(2):
                term = jnp.dot(picks[2 * i + k, :, lo:hi], slots, preferred_element_type=F32)
                term = term * cols[:, 4 * i + 2 + k:4 * i + 3 + k]
                sums[i] = term if sums[i] is None else sums[i] + term
    mine[...] = sums[1]
    swap = pltpu.make_async_remote_copy(
        src_ref=mine, dst_ref=theirs, send_sem=fs.at[3], recv_sem=fr.at[3],
        device_id=sibling, device_id_type=MESH,
    )
    swap.start()
    group_left(back, rs)
    swap.wait_recv()
    out_ref[...] = (sums[0] + theirs[...]).T[0:WIDTH].astype(BF16)
    swap.wait_send()


def on_device(grad_out, route_probs, routes, saved_up, w_up, w_down):
    vmem = pl.BlockSpec(memory_space=pltpu.VMEM)
    hbm = pl.BlockSpec(memory_space=pl.ANY)
    dma = pltpu.SemaphoreType.DMA
    message = pltpu.VMEM((CHIPS, 2 * PAIR, 128), BF16)
    slot_rows = pltpu.VMEM((SLOTS, LANES), F32)
    blocks = pltpu.VMEM((CHUNKS, 2, 4, 4, HALF, CHUNK), BF16)
    line = pltpu.VMEM((CHUNKS, 2, 4, HALF, CHUNK), BF16)
    block = pltpu.VMEM((CHUNKS, 2, HALF, CHUNK), BF16)
    flops = 2 * 2 * SLOTS * 16 * HID * WIDTH
    result = pl.pallas_call(
        kernel,
        name="experts",
        out_shape=jax.ShapeDtypeStruct((WIDTH, TOK), BF16),
        in_specs=[vmem, vmem, vmem, hbm, hbm, hbm],
        out_specs=vmem,
        scratch_shapes=[
            pltpu.VMEM((2, WIDTH, TOK), BF16),
            pltpu.VMEM((2, 2, TOK), jnp.int32),
            pltpu.VMEM((2, 2, TOK), F32),
            pltpu.VMEM((WIDTH, 16 * HID), BF16),
            pltpu.VMEM((WIDTH, 16 * HID), BF16),
            pltpu.VMEM((HID, SLOTS), BF16),
            pltpu.VMEM((16 * HID, LANES), BF16),
            message,
            message,
            message,
            message,
            slot_rows,
            slot_rows,
            blocks,
            line,
            line,
            line,
            line,
            block,
            block,
            block,
            blocks,
            pltpu.VMEM((16 * HID, CHUNK), BF16),
            slot_rows,
            pltpu.VMEM((2 * HALF, SLOTS), F32),
            pltpu.VMEM((4, TOK, SLOTS), BF16),
            pltpu.VMEM((TOK, 128), F32),
            pltpu.VMEM((TOK, LANES), F32),
            pltpu.VMEM((TOK, LANES), F32),
            dma((3,)),
            dma,
            dma((CHUNKS,)),
            dma,
            dma((CHUNKS,)),
            dma((CHUNKS, 2, 12)),
            dma((CHUNKS, 2, 12)),
            dma((4,)),
            dma((4,)),
        ],
        compiler_params=pltpu.CompilerParams(
            collective_id=0, has_side_effects=True, vmem_limit_bytes=56 * 2**20
        ),
        cost_estimate=pl.CostEstimate(flops=flops, bytes_accessed=3 * 2**20, transcendentals=0),
    )(grad_out.T, routes.T, route_probs.T, w_down[0].T, w_up[0], saved_up[0])
    return result.T


def solution(mesh):
    return jax.shard_map(
        on_device,
        mesh=mesh,
        in_specs=(
            P("tp", "ep"),
            P("tp", None),
            P("tp", None),
            P("tp", "ep", None),
            P("tp", "ep", None),
            P("tp", None, "ep"),
        ),
        out_specs=P("tp", "ep"),
        check_vma=False,
    )
```

```python
import functools
import jax
import jax.numpy as jnp
from jax import lax
from jax.experimental import pallas as pl
from jax.experimental.pallas import tpu as pltpu
from jax.sharding import PartitionSpec as P

MESH = pl.DeviceIdType.MESH
F32 = jnp.float32
BF16 = jnp.bfloat16

CHIPS = 32
AWAY = [(-(p // 2) if p % 2 == 0 else (p + 1) // 2) % CHIPS for p in range(CHIPS)]
PLACE = [AWAY.index(r) for r in range(CHIPS)]
BACK = [PLACE[-r % CHIPS] for r in AWAY]
OWN = PLACE[0]
CAP = 12
PAIR = 2 * CAP
SLOTS = CHIPS * PAIR
TOK = 256
WIDTH = 224
LANES = 256
HID = 152
HALF = 80
CHUNKS = 6
CHUNK = SLOTS // CHUNKS
READY = [0, 6, 12, 18, 24, 30]
PARTS = (0, 384, 512, 768)


def nt_dot(a, b):
    return lax.dot_general(a, b, (((1,), (1,)), ((), ())), preferred_element_type=F32)


def to_message(rows):
    n = rows.shape[0] // PAIR
    blocks = rows.reshape(n, PAIR, LANES)
    return jnp.concatenate([blocks[:, :, :128], blocks[:, :, 128:]], axis=1).astype(BF16)


def from_message(message):
    wide = message.astype(F32)
    rows = jnp.concatenate([wide[:, :PAIR], wide[:, PAIR:]], axis=2)
    return rows.reshape(rows.shape[0] * PAIR, LANES)


def look_up(table, index):
    found = jnp.zeros_like(index)
    for i, value in enumerate(table):
        found = jnp.where(index == i, value, found)
    return found


def whole(k):
    return -(-k * CHUNK // PAIR)


def done(k):
    return k * CHUNK // PAIR


def kernel(
    grad_ref, route_ref, prob_ref, down_hbm, up_hbm, saved_hbm, out_ref,
    grads, routes, probs, down_in, up, saved, down,
    send, got, back, came, x32, y32, part, in_a, in_b, in_c, run, in_a2, in_b2, in_c2, gath, gu, eg,
    factor, picks, cols, mine, theirs,
    ls, zs, zr, rs, rr, xs, xr, fs, fr,
):
    ep = lax.axis_index("ep")
    me = lax.axis_index("tp")
    z = lax.div(me, 2)
    c = lax.rem(me, 2)
    x = lax.div(ep, 4)
    y = lax.rem(ep, 4)
    s = 1 - 2 * c
    sibling = (ep, 2 * z + 1 - c)

    def chip(r):
        return (ep, lax.rem(z + r, CHIPS) * 2 + c)

    def near(o, phase, coord):
        along_x = (o == 0) == (phase == 0)
        return (coord * 4 + y if along_x else x * 4 + coord, me)

    def ring(coord):
        return lax.rem(coord + s + 4, 4), lax.rem(coord - s + 4, 4), lax.rem(coord + 2, 4)

    barrier = pltpu.get_barrier_semaphore()

    def greet(r, carry):
        pl.semaphore_signal(barrier, inc=1, device_id=chip(r), device_id_type=MESH)
        return carry

    lax.fori_loop(1, CHIPS, greet, 0)
    pl.semaphore_signal(barrier, inc=1, device_id=sibling, device_id_type=MESH)
    for o in range(2):
        for step in (1, 2, 3):
            peer = near(o, 0, lax.rem((x if o == 0 else y) + step, 4))
            pl.semaphore_signal(barrier, inc=1, device_id=peer, device_id_type=MESH)
    loads = [
        pltpu.make_async_copy(src, dst, ls.at[i])
        for i, (src, dst) in enumerate([(down_hbm, down_in), (saved_hbm, saved), (up_hbm, up)])
    ]
    for load in loads:
        load.start()
    pl.semaphore_wait(barrier, CHIPS - 1 + 1 + 6)

    trades = [
        pltpu.make_async_remote_copy(
            src_ref=src, dst_ref=dst.at[c], send_sem=fs.at[i], recv_sem=fr.at[i],
            device_id=sibling, device_id_type=MESH,
        )
        for i, (src, dst) in enumerate([(route_ref, routes), (prob_ref, probs), (grad_ref, grads)])
    ]
    for trade in trades:
        trade.start()
    grads[c] = grad_ref[...]
    routes[c] = route_ref[...]
    probs[c] = prob_ref[...]

    expert = lax.broadcasted_iota(jnp.int32, (64, 1), 0)
    away = ((expert >> 1) - z + CHIPS) & (CHIPS - 1)
    place_to = look_up(PLACE, away)
    place_from = look_up(BACK, place_to)
    base_to = jnp.where((expert & 1) == c, place_to * PAIR, -4096).astype(F32)
    base_from = jnp.where((expert & 1) == c, place_from * PAIR, -4096).astype(F32)
    experts = lax.broadcasted_iota(jnp.int32, (64, TOK), 0)
    earlier = jnp.where(
        lax.broadcasted_iota(jnp.int32, (TOK, TOK), 0) < lax.broadcasted_iota(jnp.int32, (TOK, TOK), 1),
        1.0, 0.0,
    ).astype(BF16)
    rows = lax.broadcasted_iota(jnp.int32, (SLOTS, TOK), 0).astype(F32)

    def tokens_of(block):
        route = routes[block]
        first = jnp.where(experts == route[0:1], 1.0, 0.0)
        second = jnp.where(experts == route[1:2], 1.0, 0.0)
        before = jnp.dot((first + second).astype(BF16), earlier, preferred_element_type=F32)
        shift = (CAP * block).astype(F32)
        one, two, one_from, two_from = [
            jnp.sum(hot * (before + base), axis=0, keepdims=True) + shift
            for base in (base_to, base_from)
            for hot in (first, second)
        ]
        hot = jnp.where((rows == one) | (rows == two), 1.0, 0.0).astype(BF16)
        wide = jnp.concatenate([grads[block], jnp.zeros((LANES - WIDTH, TOK), BF16)], axis=0)
        return nt_dot(hot, wide), [one_from, two_from, probs[block]]

    total, found = tokens_of(c)
    for trade in trades:
        trade.wait_recv()
    other, other_found = tokens_of(1 - c)
    send[...] = to_message(total + other)

    def dispatch(p, group):
        i = BACK[p]
        return pltpu.make_async_remote_copy(
            src_ref=send.at[i], dst_ref=got.at[p], send_sem=zs, recv_sem=zr.at[group],
            device_id=chip(AWAY[i]), device_id_type=MESH,
        )

    def send_back(p, group):
        return pltpu.make_async_remote_copy(
            src_ref=back.at[p], dst_ref=came.at[p], send_sem=rs, recv_sem=rr.at[group],
            device_id=chip(AWAY[p]), device_id_type=MESH,
        )

    def each_place(lo, hi, act):
        for p in range(lo, hi):
            if p != OWN:
                act(p)

    def group_ref(buffer, lo, hi):
        return buffer.at[lo:hi - (1 if lo <= OWN < hi else 0)]

    def group_arrived(buffer, lo, hi, sem):
        ref = group_ref(buffer, lo, hi)
        pltpu.make_async_remote_copy(
            src_ref=ref, dst_ref=ref, send_sem=zs, recv_sem=sem, device_id=sibling, device_id_type=MESH,
        ).wait_recv()

    def group_left(buffer, sem):
        ref = group_ref(buffer, 0, CHIPS)
        pltpu.make_async_remote_copy(
            src_ref=ref, dst_ref=ref, send_sem=sem, recv_sem=zr.at[0], device_id=sibling, device_id_type=MESH,
        ).wait_send()

    for k in range(CHUNKS):
        each_place(whole(k), whole(k + 1), lambda p, k=k: dispatch(p, k).start())
    got[OWN] = send[OWN]

    loads[0].wait()

    def turn(j, carry):
        at = pl.multiple_of(128 * j, 128)
        block = down_in[:, pl.ds(at, 128)].astype(F32)
        block = jnp.concatenate([block, jnp.zeros((LANES - WIDTH, 128), F32)], axis=0)
        down[pl.ds(at, 128), :] = block.T.astype(BF16)
        return carry

    lax.fori_loop(0, 16 * HID // 128, turn, 0)
    def make_factor():
        loads[1].wait()
        lane = lax.broadcasted_iota(jnp.int32, (1, SLOTS), 1)
        place = (lane * 2731) >> 16
        source = ((z + look_up(AWAY, place)) & (CHIPS - 1)) * PAIR + (lane - PAIR * place)
        order = jnp.where(
            lax.broadcasted_iota(jnp.int32, (SLOTS, SLOTS), 0) == source, 1.0, 0.0
        ).astype(BF16)
        u = jnp.dot(saved[...], order, preferred_element_type=F32)
        g = 1.0 / (1.0 + jnp.exp(-u))
        factor[0:HID] = g * (1.0 + u * (1.0 - g))
        factor[HID:] = jnp.zeros((2 * HALF - HID, SLOTS), F32)

    def make_picks():
        cols[...] = jnp.concatenate(found + other_found + [jnp.zeros((120, TOK), F32)], axis=0).T
        lanes = lax.broadcasted_iota(jnp.int32, (TOK, SLOTS), 1).astype(F32)
        for i, column in enumerate((0, 1, 4, 5)):
            picks[i] = jnp.where(lanes == cols[:, column:column + 1], 1.0, 0.0).astype(BF16)

    def transfers(k, o):
        a, b = (x, y) if o == 0 else (y, x)
        ap, am, a2 = ring(a)
        bp, bm, b2 = ring(b)
        ga = gath.at[k, o]
        return [
            (part.at[k, o, a2], in_a.at[k, o], near(o, 0, ap), in_a.at[k, o]),
            (part.at[k, o, am], in_b.at[k, o], near(o, 0, am), in_b.at[k, o]),
            (part.at[k, o, ap], in_c.at[k, o], near(o, 0, ap), in_c.at[k, o]),
            (run.at[k, o, bp], in_a2.at[k, o], near(o, 1, bp), in_a2.at[k, o]),
            (run.at[k, o, bm], in_b2.at[k, o], near(o, 1, bm), in_b2.at[k, o]),
            (run.at[k, o, b2], in_c2.at[k, o], near(o, 1, b2), in_c2.at[k, o]),
            (ga.at[a, b], ga.at[a, b], near(o, 1, bp), ga.at[a, bm]),
            (ga.at[a, b], ga.at[a, b], near(o, 1, bm), ga.at[a, bp]),
            (ga.at[a, b], ga.at[a, b], near(o, 1, b2), ga.at[a, b2]),
            (ga.at[a], ga.at[a], near(o, 0, ap), ga.at[am]),
            (ga.at[a], ga.at[a], near(o, 0, am), ga.at[ap]),
            (ga.at[am], ga.at[am], near(o, 0, ap), ga.at[a2]),
        ]

    def link(k, o, q, src, dst, peer):
        return pltpu.make_async_remote_copy(
            src_ref=src, dst_ref=dst, send_sem=xs.at[k, o, q], recv_sem=xr.at[k, o, q],
            device_id=peer, device_id_type=MESH,
        )

    def start(k, o, *qs):
        for q in qs:
            src, dst, peer, _ = transfers(k, o)[q]
            link(k, o, q, src, dst, peer).start()

    def arrived(k, o, *qs):
        for q in qs:
            _, _, peer, land = transfers(k, o)[q]
            link(k, o, q, land, land, peer).wait_recv()

    def left(k, o, *qs):
        for q in qs:
            src, dst, peer, _ = transfers(k, o)[q]
            link(k, o, q, src, dst, peer).wait_send()

    def stage0(k):
        lo, hi = whole(k), whole(k + 1)
        group_arrived(got, lo, hi, zr.at[k])
        x32[PAIR * lo:PAIR * hi] = from_message(got[lo:hi])
        tokens = x32[k * CHUNK:(k + 1) * CHUNK].astype(BF16)

        def pair(i, carry):
            weights = down[pl.ds(pl.multiple_of(2 * HID * i, 16), 2 * HID), :]
            hidden = nt_dot(weights, tokens)
            px = lax.div(i, 2)
            for j in range(2):
                py = 2 * lax.rem(i, 2) + j
                block = hidden[j * HID:(j + 1) * HID]
                part[k, 0, px, py] = block[0:HALF].astype(BF16)
                part[k, 1, py, px] = jnp.concatenate(
                    [block[HALF:], jnp.zeros((2 * HALF - HID, CHUNK), F32)], axis=0
                ).astype(BF16)
            return carry

        lax.fori_loop(0, 8, pair, 0)
        for o in range(2):
            start(k, o, 0, 1)

    def stage1(k):
        for o in range(2):
            ap, _, _ = ring(x if o == 0 else y)
            arrived(k, o, 0)
            part[k, o, ap] = (part[k, o, ap].astype(F32) + in_a[k, o].astype(F32)).astype(BF16)
            start(k, o, 2)

    def stage2(k):
        for o in range(2):
            arrived(k, o, 1, 2)
            a = x if o == 0 else y
            run[k, o] = (
                part[k, o, a].astype(F32) + in_b[k, o].astype(F32) + in_c[k, o].astype(F32)
            ).astype(BF16)
            start(k, o, 3, 4, 5)

    def stage3(k):
        for o in range(2):
            arrived(k, o, 3, 4, 5)
            a, b = (x, y) if o == 0 else (y, x)
            hidden = run[k, o, b].astype(F32) + in_a2[k, o].astype(F32)
            hidden = hidden + in_b2[k, o].astype(F32) + in_c2[k, o].astype(F32)
            slope = factor[o * HALF:(o + 1) * HALF, k * CHUNK:(k + 1) * CHUNK]
            gath[k, o, a, b] = (hidden * slope).astype(BF16)
            start(k, o, 6, 7, 8)

    def stage4(k):
        for o in range(2):
            arrived(k, o, 6, 7, 8)
            start(k, o, 9, 10)

    def stage5(k):
        for o in range(2):
            arrived(k, o, 9)
            start(k, o, 11)

    def stage6(k):
        for o in range(2):
            arrived(k, o, 10, 11)

        def pair(i, carry):
            px = lax.div(i, 2)
            pieces = []
            for j in range(2):
                py = 2 * lax.rem(i, 2) + j
                pieces.append(gath[k, 0, px, py].astype(F32))
                pieces.append(gath[k, 1, py, px].astype(F32)[0:HID - HALF])
            gu[pl.ds(pl.multiple_of(2 * HID * i, 16), 2 * HID), :] = jnp.concatenate(pieces, axis=0).astype(BF16)
            return carry

        lax.fori_loop(0, 8, pair, 0)
        result = jnp.dot(up[...], gu[...], preferred_element_type=F32)
        padded = jnp.concatenate([result, jnp.zeros((LANES - WIDTH, CHUNK), F32)], axis=0)
        eg[k * CHUNK:(k + 1) * CHUNK] = padded.T
        lo, hi = done(k), done(k + 1)
        back[lo:hi] = to_message(eg[PAIR * lo:PAIR * hi])
        each_place(lo, hi, lambda p: send_back(p, k).start())
        if lo <= OWN < hi:
            came[OWN] = back[OWN]

    stages = [stage0, stage1, stage2, stage3, stage4, stage5, stage6]
    offsets = [0, 4, 7, 10.5, 13.5, 17.5, 20.5]
    plan = sorted((READY[k] + offsets[i], k, i) for k in range(CHUNKS) for i in range(len(stages)))
    for _, k, i in plan:
        stages[i](k)
        if (k, i) == (0, 0):
            make_factor()
        if (k, i) == (0, 1):
            make_picks()
            loads[2].wait()
    group_left(send, zs)
    for k in range(CHUNKS):
        for o in range(2):
            left(k, o, *range(12))
    for trade in trades:
        trade.wait_send()

    sums = [None, None]
    taken = 0
    for lo, hi in zip(PARTS[:-1], PARTS[1:]):
        while done(taken) * PAIR < hi:
            first, last = done(taken), done(taken + 1)
            group_arrived(came, first, last, rr.at[taken])
            y32[PAIR * first:PAIR * last] = from_message(came[first:last])
            taken += 1
        slots = y32[lo:hi].astype(BF16)
        for i in range(2):
            for k in range(2):
                term = jnp.dot(picks[2 * i + k, :, lo:hi], slots, preferred_element_type=F32)
                term = term * cols[:, 4 * i + 2 + k:4 * i + 3 + k]
                sums[i] = term if sums[i] is None else sums[i] + term
    mine[...] = sums[1]
    swap = pltpu.make_async_remote_copy(
        src_ref=mine, dst_ref=theirs, send_sem=fs.at[3], recv_sem=fr.at[3],
        device_id=sibling, device_id_type=MESH,
    )
    swap.start()
    group_left(back, rs)
    swap.wait_recv()
    out_ref[...] = (sums[0] + theirs[...]).T[0:WIDTH].astype(BF16)
    swap.wait_send()


def on_device(grad_out, route_probs, routes, saved_up, w_up, w_down):
    vmem = pl.BlockSpec(memory_space=pltpu.VMEM)
    hbm = pl.BlockSpec(memory_space=pl.ANY)
    dma = pltpu.SemaphoreType.DMA
    message = pltpu.VMEM((CHIPS, 2 * PAIR, 128), BF16)
    slot_rows = pltpu.VMEM((SLOTS, LANES), F32)
    blocks = pltpu.VMEM((CHUNKS, 2, 4, 4, HALF, CHUNK), BF16)
    line = pltpu.VMEM((CHUNKS, 2, 4, HALF, CHUNK), BF16)
    block = pltpu.VMEM((CHUNKS, 2, HALF, CHUNK), BF16)
    flops = 2 * 2 * SLOTS * 16 * HID * WIDTH
    result = pl.pallas_call(
        kernel,
        name="experts",
        out_shape=jax.ShapeDtypeStruct((WIDTH, TOK), BF16),
        in_specs=[vmem, vmem, vmem, hbm, hbm, hbm],
        out_specs=vmem,
        scratch_shapes=[
            pltpu.VMEM((2, WIDTH, TOK), BF16),
            pltpu.VMEM((2, 2, TOK), jnp.int32),
            pltpu.VMEM((2, 2, TOK), F32),
            pltpu.VMEM((WIDTH, 16 * HID), BF16),
            pltpu.VMEM((WIDTH, 16 * HID), BF16),
            pltpu.VMEM((HID, SLOTS), BF16),
            pltpu.VMEM((16 * HID, LANES), BF16),
            message,
            message,
            message,
            message,
            slot_rows,
            slot_rows,
            blocks,
            line,
            line,
            line,
            line,
            block,
            block,
            block,
            blocks,
            pltpu.VMEM((16 * HID, CHUNK), BF16),
            slot_rows,
            pltpu.VMEM((2 * HALF, SLOTS), F32),
            pltpu.VMEM((4, TOK, SLOTS), BF16),
            pltpu.VMEM((TOK, 128), F32),
            pltpu.VMEM((TOK, LANES), F32),
            pltpu.VMEM((TOK, LANES), F32),
            dma((3,)),
            dma,
            dma((CHUNKS,)),
            dma,
            dma((CHUNKS,)),
            dma((CHUNKS, 2, 12)),
            dma((CHUNKS, 2, 12)),
            dma((4,)),
            dma((4,)),
        ],
        compiler_params=pltpu.CompilerParams(
            collective_id=0, has_side_effects=True, vmem_limit_bytes=56 * 2**20
        ),
        cost_estimate=pl.CostEstimate(flops=flops, bytes_accessed=3 * 2**20, transcendentals=0),
    )(grad_out.T, routes.T, route_probs.T, w_down[0].T, w_up[0], saved_up[0])
    return result.T


def solution(mesh):
    return jax.shard_map(
        on_device,
        mesh=mesh,
        in_specs=(
            P("tp", "ep"),
            P("tp", None),
            P("tp", None),
            P("tp", "ep", None),
            P("tp", "ep", None),
            P("tp", None, "ep"),
        ),
        out_specs=P("tp", "ep"),
        check_vma=False,
    )
```
